512 devices in a mesh: node: 8 (over y_hi, core), dp: 64 (over z, y_lo, x).
Axes of the slice: x: 4, y: 8 (y_hi: 4, y_lo: 2; y = y_hi * 2 + y_lo), z: 8, core: 2. Of those that a mesh axis runs over, the one named last changes fastest.
Arguments:
- hidden: bfloat16 [64, 1024, 13824], P('dp', 'node'), may hold values from -6 to 6
- cotangent: bfloat16 [64, 1024, 16], P('dp', 'node'), may hold values from -0.1875 to 0.1875
- momentum: float32 [64, 16, 13824], P('dp', 'node'), may hold values from -6 to 6
- worker_error: float32 [64, 16, 13824], P('dp', 'node'), may hold values from -1.8 to 1.8
- server_error: float32 [16, 13824], P('node', 'dp'), may hold values from -0.3 to 0.3
- master: float32 [16, 13824], P('node'), may hold values from -3 to 3
- second_moment: float32 [16, 13824], P('node'), may hold values from 0.0004 to 0.01
Outputs:
- moment: float32 [64, 16, 13824], P('dp', 'node')
- new_worker_error: float32 [64, 16, 13824], P('dp', 'node')
- new_server_error: float32 [16, 13824], P('node', 'dp')
- weights: bfloat16 [16, 13824], replicated
The draws below stay inside these ranges and needn't reach their ends.
All inputs are finite; a program needn't handle non-finite values.
Results may differ from the reference program's by a relative error of at most 0.0085.
Values may be sent and summed in bfloat16 or wider, within the bound.
A program may use at most 64 MiB of HBM per device.

```python
import math
import jax
import jax.numpy as jnp
from jax import lax

FF = 13824
ROWS = 16
NODE_TOK = 1024
REPLICAS = 64
N_NODE = 8
N_DP = 64


def steps_of(own_key, dims, cuts, smallest, high):
    def one(position, shards_of):
        steps = jax.random.uniform(jax.random.fold_in(jax.random.fold_in(own_key, 6), position), (shards_of,), jnp.float32, smallest / len(cuts), high / len(cuts))
        return jnp.repeat(jnp.exp(steps), dims[position] // shards_of).reshape((-1,) + (1,) * (len(dims) - position - 1))

    level = one(*cuts[0])
    for cut in cuts[1:]:
        level = level * one(*cut)
    return level


def noise(key, dims, width, limit, cuts=(), held_as=jnp.bfloat16):
    factor_of = steps_of(key, dims, cuts, -0.22, 0.18) if cuts else 1.0
    result = jax.random.normal(key, dims, jnp.float32) * width * factor_of
    return jnp.minimum(jnp.maximum(result, -limit), limit).astype(held_as)


def setup_inputs(seed: int = 0) -> dict:
    splits = jax.random.split(jax.random.key(seed), 8)
    return {
        "hidden": noise(splits[0], (REPLICAS, NODE_TOK, FF), 1.0, 6.0, ((0, 64), (1, 8))),
        "cotangent": noise(splits[1], (REPLICAS, NODE_TOK, ROWS), (1.0 / NODE_TOK ** 0.5), 0.1875, ((0, 64), (1, 8))),
        "momentum": noise(splits[2], (REPLICAS, ROWS, FF), 1.0, 6.0, ((0, 64), (1, 8)), jnp.float32),
        "worker_error": noise(splits[3], (REPLICAS, ROWS, FF), 0.3, 1.8, ((0, 64), (1, 8)), jnp.float32),
        "server_error": noise(splits[4], (ROWS, FF), 0.05, 0.3, ((0, 8), (1, 64)), jnp.float32),
        "master": noise(splits[5], (ROWS, FF), 0.5, 3.0, ((0, 8),), jnp.float32),
        "second_moment": jnp.clip(jnp.exp(math.log(0.01) - 3.218876 * jax.random.uniform(splits[6], (ROWS, FF), jnp.float32) ** steps_of(splits[6], (ROWS, FF), ((0, 8),), -0.2, 0.2)), 0.0004, 0.01),
    }


beta_one = 0.9
epsilon = 1e-06
learn_rate = 0.5

def replica_gradient(pair):
    cotan, acts = pair
    return jnp.dot(cotan.T, acts, preferred_element_type=jnp.float32)

def reference(hidden, cotangent, momentum, worker_error, server_error, master, second_moment):
    gradient = lax.map(replica_gradient, (cotangent, hidden))
    moment = beta_one * momentum + (1.0 - beta_one) * gradient
    carried = moment + worker_error
    blocks = carried.reshape(N_DP, N_NODE, ROWS // N_NODE, FF)
    worker_scale = jnp.sqrt(lax.optimization_barrier(jnp.mean(blocks * blocks, axis=(2, 3), keepdims=True)) + epsilon)
    sent = (worker_scale * jnp.tanh(blocks / worker_scale)).astype(jnp.bfloat16)
    new_worker = (blocks - sent.astype(jnp.float32)).reshape(N_DP, ROWS, FF)
    average = lax.optimization_barrier(jnp.sum(sent.astype(jnp.float32), axis=0)) / N_DP
    served = average.reshape(ROWS, FF) + server_error
    pieces = served.reshape(N_NODE, ROWS // N_NODE, N_DP, FF // N_DP)
    server_scale = jnp.sqrt(lax.optimization_barrier(jnp.mean(pieces * pieces, axis=(1, 3), keepdims=True)) + epsilon)
    returned = (server_scale * jnp.tanh(pieces / server_scale)).astype(jnp.bfloat16)
    new_server = (pieces - returned.astype(jnp.float32)).reshape(ROWS, FF)
    update = returned.astype(jnp.float32).reshape(ROWS, FF) / (jnp.sqrt(second_moment) + 1e-08)
    weights = (master - learn_rate * update).astype(jnp.bfloat16)
    return (moment, new_worker, new_server, weights)
```

```python
import functools

import jax
import jax.numpy as jnp
from jax import lax
from jax.experimental import pallas as pl
from jax.experimental.pallas import tpu as pltpu
from jax.sharding import PartitionSpec as P

MESH = pl.DeviceIdType.MESH
F32 = jnp.float32
BF16 = jnp.bfloat16

FF = 13824
LANES = 128
GROUPS = FF // LANES
DENSE = 2 * GROUPS
PADDED = 224
SERVERS = 64
PIECE = FF // SERVERS
QUARTER = GROUPS // 4
BETA = 0.9
EPSILON = 1e-6
RATE = 0.5


def far_first(j, half):
    odd = lax.rem(j, 2)
    return half + (1 - odd) * (j // 2) - odd * ((j + 1) // 2)


def device(x, y, z, c):
    return ((y // 2) * 2 + c, z * 8 + lax.rem(y, 2) * 4 + x)


def kernel(
    hid, cot, mom, werr, serr, mast, second,
    moment_out, werr_out, serr_out, weights_out,
    hid_v, part, core_in, y_out, y_in, mom_v, werr_v, mast_v, second_v, serr_v,
    sent_v, pieces, arrived, wpiece, gathered, wall, spread,
    load_sem, store_sem, core_send, core_recv, y_send, y_recv, ready,
    b_send, b_recv, c_send, c_recv, x_send, x_recv, s_send, s_recv,
):
    node = lax.axis_index("node")
    dp = lax.axis_index("dp")
    c = lax.rem(node, 2)
    yh = node // 2
    z = dp // 8
    yl = lax.rem(dp // 4, 2)
    x = lax.rem(dp, 4)
    y = yh * 2 + yl
    sibling = (node + 1 - 2 * c, dp)

    loads = [
        pltpu.make_async_copy(
            hid.at[:, pl.ds(j * QUARTER * LANES, QUARTER * LANES)],
            hid_v.at[:, pl.ds(j * QUARTER * LANES, QUARTER * LANES)],
            load_sem.at[j],
        )
        for j in range(4)
    ]
    states = [
        pltpu.make_async_copy(mom.reshape(DENSE, LANES), mom_v.at[pl.ds(0, DENSE)], load_sem.at[4]),
        pltpu.make_async_copy(werr.reshape(DENSE, LANES), werr_v.at[pl.ds(0, DENSE)], load_sem.at[5]),
        pltpu.make_async_copy(mast, mast_v.at[pl.ds(0, GROUPS)], load_sem.at[6]),
        pltpu.make_async_copy(second, second_v.at[pl.ds(0, GROUPS)], load_sem.at[7]),
    ]
    for load in loads:
        load.start()

    barrier = pltpu.get_barrier_semaphore()

    def greet(who):
        pl.semaphore_signal(barrier, 1, device_id=who, device_id_type=MESH)

    @pl.loop(0, 7)
    def _(j):
        greet(device(x, y, lax.rem(z + far_first(j, 4), 8), c))
        greet(device(x, lax.rem(y + far_first(j, 4), 8), z, c))

    @pl.loop(1, 4)
    def _(j):
        other = lax.rem(x + j, 4)
        greet(device(other, y, z, c))
        greet(device(other, yh * 2 + 1 - yl, z, c))

    greet(sibling)

    for state in states:
        state.start()

    tail = jnp.zeros((PADDED - DENSE, LANES), F32)
    for a in range(2):
        for b in range(4):
            part[a, b, pl.ds(DENSE, PADDED - DENSE), :] = tail
    mom_v[pl.ds(DENSE, PADDED - DENSE), :] = tail
    werr_v[pl.ds(DENSE, PADDED - DENSE), :] = tail
    mast_v[pl.ds(GROUPS, 4)] = jnp.zeros((4, 2, LANES), F32)
    second_v[pl.ds(GROUPS, 4)] = jnp.zeros((4, 2, LANES), F32)
    serr_v[...] = jnp.zeros((4, LANES), F32)
    serr_v[pl.ds(0, 2), :] = serr[:, pl.ds(0, LANES)]
    serr_v[pl.ds(2, 2), pl.ds(0, PIECE - LANES)] = serr[:, pl.ds(LANES, PIECE - LANES)]

    cot_value = cot[...]
    for j in range(4):
        loads[j].wait()
        sums = jnp.dot(
            cot_value,
            hid_v[:, pl.ds(j * QUARTER * LANES, QUARTER * LANES)],
            preferred_element_type=F32,
        )
        for g in range(QUARTER):
            row = 2 * (j * QUARTER + g)
            for n in range(8):
                part[n % 2, n // 2, pl.ds(row, 2), :] = sums[
                    2 * n : 2 * n + 2, g * LANES : (g + 1) * LANES
                ]

    pl.semaphore_wait(barrier, 21)

    def to_core(d):
        return pltpu.make_async_remote_copy(
            part.at[1 - c, lax.rem(yh + d, 4)], core_in.at[d], core_send.at[d], core_recv.at[d],
            device_id=sibling, device_id_type=MESH,
        )

    def to_node(d):
        return pltpu.make_async_remote_copy(
            y_out.at[d - 1], y_in.at[d - 1], y_send.at[d - 1], y_recv.at[d - 1],
            device_id=(lax.rem(yh + d, 4) * 2 + c, dp), device_id_type=MESH,
        )

    for d in (2, 1, 3, 0):
        to_core(d).start()

    @pl.loop(0, 7)
    def _(j):
        pl.semaphore_signal(
            ready, 1, device_id=device(x, y, lax.rem(z + far_first(j, 4), 8), c), device_id_type=MESH
        )

    for d in (2, 1, 3):
        to_core(d).wait_recv()
        y_out[d - 1] = (part[c, lax.rem(yh + d, 4)] + core_in[d]).astype(BF16)
        to_node(d).start()
    to_core(0).wait_recv()
    gradient = part[c, yh] + core_in[0]
    states[0].wait()
    states[1].wait()
    for d in (1, 3, 2):
        to_node(d).wait_recv()
        gradient = gradient + y_in[d - 1].astype(F32)

    moment = BETA * mom_v[...] + (1.0 - BETA) * gradient
    carried = moment + werr_v[...]
    mom_v[...] = moment
    square = jnp.sum(carried * carried, axis=(0, 1), keepdims=True)
    scale = jnp.sqrt(square / (2 * FF) + EPSILON)
    sent = (scale * jnp.tanh(carried / scale)).astype(BF16).astype(F32)
    sent_v[...] = sent
    werr_v[...] = carried - sent

    lane = lax.broadcasted_iota(jnp.int32, (8, LANES), 1)
    for p in range(SERVERS):
        group, shift = divmod(PIECE * p, LANES)
        rows = sent_v[pl.ds(2 * group, 8), :]
        if shift:
            first = pltpu.roll(rows, LANES - shift, 1)
            rows = jnp.where(lane < LANES - shift, first, pltpu.roll(first, 6, 0))
        pieces[p] = rows[0:4]

    pl.semaphore_wait(ready, 7)

    def to_server(k):
        jz, jx, jy = k // 8, lax.rem(k, 8) // 2, lax.rem(k, 2)
        tz = lax.rem(z + far_first(jz, 4), 8)
        tx = lax.rem(x + far_first(jx, 2), 4)
        ty = lax.rem(yl + 1 - jy, 2)
        target = tz * 8 + ty * 4 + tx
        return pltpu.make_async_remote_copy(
            pieces.at[target], arrived.at[dp], b_send, b_recv, device_id=(node, target), device_id_type=MESH
        )

    @pl.loop(0, SERVERS - 1)
    def _(k):
        to_server(k).start()

    arrived[dp] = pieces[dp]
    moment_store = pltpu.make_async_copy(mom_v.at[pl.ds(0, DENSE)], moment_out.reshape(DENSE, LANES), store_sem.at[0])
    werr_store = pltpu.make_async_copy(werr_v.at[pl.ds(0, DENSE)], werr_out.reshape(DENSE, LANES), store_sem.at[1])
    moment_store.start()
    werr_store.start()

    states[2].wait()
    states[3].wait()
    column = dp * PIECE
    group, shift = column // LANES, lax.rem(column, LANES)

    def own_piece(ref):
        rows = jnp.concatenate([ref[group + j] for j in range(4)], axis=0)
        first = pltpu.roll(rows, lax.rem(LANES - shift, LANES), 1)
        return jnp.where(lane < LANES - shift, first, pltpu.roll(first, 6, 0))[0:4]

    row4 = lax.broadcasted_iota(jnp.int32, (4, LANES), 0)
    lane4 = lax.broadcasted_iota(jnp.int32, (4, LANES), 1)
    valid = (row4 < 2) | (lane4 < PIECE - LANES)
    own_master = own_piece(mast_v)
    divisor = jnp.sqrt(jnp.where(valid, own_piece(second_v), 1.0)) + 1e-8

    everyone = SERVERS - 1
    pltpu.make_async_copy(pieces.at[pl.ds(0, everyone)], arrived.at[pl.ds(0, everyone)], b_recv).wait()
    served = jnp.sum(arrived[...], axis=0) / SERVERS + serr_v[...]
    served = jnp.where(valid, served, 0.0)
    square = jnp.sum(served * served, axis=(0, 1), keepdims=True)
    scale = jnp.sqrt(square / (2 * PIECE) + EPSILON)
    returned = (scale * jnp.tanh(served / scale)).astype(BF16).astype(F32)
    updated = own_master - RATE * (returned / divisor)
    updated = jnp.concatenate([updated[0:1], updated[2:3], updated[1:2], updated[3:4]], axis=0)
    wpiece[...] = updated.astype(BF16).astype(F32)

    slot = (z * 2 + yl) * 4 + yh

    def to_plane(k):
        tz = lax.rem(z + far_first(k // 8, 4), 8)
        ty = lax.rem(y + far_first(lax.rem(k, 8), 4), 8)
        return pltpu.make_async_remote_copy(
            wpiece, gathered.at[slot], c_send, c_recv, device_id=device(x, ty, tz, c), device_id_type=MESH
        )

    @pl.loop(0, SERVERS - 1)
    def _(k):
        to_plane(k).start()

    gathered[slot] = wpiece[...]
    residual = served - returned
    serr_out[:, pl.ds(0, LANES)] = residual[0:2]
    serr_out[:, pl.ds(LANES, PIECE - LANES)] = residual[2:4, 0 : PIECE - LANES]

    pltpu.make_async_copy(pieces.at[pl.ds(0, everyone)], gathered.at[pl.ds(0, everyone)], c_recv).wait()
    wall[c, x] = gathered[...].reshape(4 * SERVERS, LANES).astype(BF16)

    def to_x(d):
        return pltpu.make_async_remote_copy(
            wall.at[c, x], wall.at[c, x], x_send.at[d - 1], x_recv.at[d - 1],
            device_id=(node, dp - x + lax.rem(x + d, 4)), device_id_type=MESH,
        )

    def from_x(d):
        block = wall.at[c, lax.rem(x + 4 - d, 4)]
        return pltpu.make_async_remote_copy(
            block, block, x_send.at[d - 1], x_recv.at[d - 1],
            device_id=(node, dp - x + lax.rem(x + d, 4)), device_id_type=MESH,
        )

    def to_sibling(d):
        block = wall.at[c, lax.rem(x + 4 - d, 4)]
        return pltpu.make_async_remote_copy(
            block, block, s_send.at[d], s_recv.at[d], device_id=sibling, device_id_type=MESH
        )

    def from_sibling(d):
        block = wall.at[1 - c, lax.rem(x + 4 - d, 4)]
        return pltpu.make_async_remote_copy(
            block, block, s_send.at[d], s_recv.at[d], device_id=sibling, device_id_type=MESH
        )

    for d in (2, 1, 3):
        to_x(d).start()
    to_sibling(0).start()
    for d in (1, 3, 2):
        from_x(d).wait_recv()
        to_sibling(d).start()
    for d in (0, 1, 3, 2):
        from_sibling(d).wait_recv()

    @pl.loop(0, 4)
    def _(q):
        parts = [[] for _ in range(QUARTER)]
        for pp in range(16):
            for core in range(2):
                block = wall[core, pp % 4, pl.ds(pl.multiple_of(q * 64 + 16 * (pp // 4), 16), 16), :].astype(F32)
                for h in range(4):
                    spread[pp, pl.ds(8 * h + 4 * core, 4), :] = block[4 * h : 4 * h + 4]
            for half in range(2):
                rows = [spread[pp, pl.ds(16 * h + half, 8, stride=2), :] for h in range(2)]
                begin = PIECE * pp + LANES * half
                end = min(begin + LANES, PIECE * (pp + 1))
                group, shift = divmod(begin, LANES)
                if shift:
                    rows = [pltpu.roll(r, shift, 1) for r in rows]
                for g in (group, group + 1):
                    if max(begin, g * LANES) < min(end, (g + 1) * LANES):
                        parts[g].append((max(begin, g * LANES) - g * LANES, rows))
        for g in range(QUARTER):
            total = parts[g][0][1]
            for low, rows in parts[g][1:]:
                total = [jnp.where(lane < low, t, r) for t, r in zip(total, rows)]
            weights_out[:, pl.ds(pl.multiple_of(q * QUARTER * LANES + g * LANES, LANES), LANES)] = (
                jnp.concatenate(total, axis=0).astype(BF16)
            )

    moment_store.wait()
    werr_store.wait()
    for d in range(4):
        to_core(d).wait_send()
        to_sibling(d).wait_send()
    for d in range(1, 4):
        to_node(d).wait_send()
        to_x(d).wait_send()
    pltpu.make_async_copy(pieces.at[pl.ds(0, everyone)], arrived.at[pl.ds(0, everyone)], b_send).wait()
    pltpu.make_async_copy(pieces.at[pl.ds(0, everyone)], gathered.at[pl.ds(0, everyone)], c_send).wait()


def grouped(a):
    return a.reshape(2, GROUPS, LANES).transpose(1, 0, 2)


def body(hidden, cotangent, momentum, worker_error, server_error, master, second_moment):
    anywhere = pl.BlockSpec(memory_space=pl.ANY)
    vmem = pl.BlockSpec(memory_space=pltpu.VMEM)
    dma = pltpu.SemaphoreType.DMA
    moment, werr, serr, weights = pl.pallas_call(
        kernel,
        out_shape=[
            jax.ShapeDtypeStruct((GROUPS, 2, LANES), F32),
            jax.ShapeDtypeStruct((GROUPS, 2, LANES), F32),
            jax.ShapeDtypeStruct((2, PIECE), F32),
            jax.ShapeDtypeStruct((16, FF), BF16),
        ],
        in_specs=[anywhere, vmem, anywhere, anywhere, vmem, anywhere, anywhere],
        out_specs=[anywhere, anywhere, vmem, vmem],
        scratch_shapes=[
            pltpu.VMEM((128, FF), BF16),
            pltpu.VMEM((2, 4, PADDED, LANES), F32),
            pltpu.VMEM((4, PADDED, LANES), F32),
            pltpu.VMEM((3, PADDED, LANES), BF16),
            pltpu.VMEM((3, PADDED, LANES), BF16),
            pltpu.VMEM((PADDED, LANES), F32),
            pltpu.VMEM((PADDED, LANES), F32),
            pltpu.VMEM((GROUPS + 4, 2, LANES), F32),
            pltpu.VMEM((GROUPS + 4, 2, LANES), F32),
            pltpu.VMEM((4, LANES), F32),
            pltpu.VMEM((PADDED, LANES), F32),
            pltpu.VMEM((SERVERS, 4, LANES), F32),
            pltpu.VMEM((SERVERS, 4, LANES), F32),
            pltpu.VMEM((4, LANES), F32),
            pltpu.VMEM((SERVERS, 4, LANES), F32),
            pltpu.VMEM((2, 4, 4 * SERVERS, LANES), BF16),
            pltpu.VMEM((16, 32, LANES), F32),
            dma((8,)), dma((2,)), dma((4,)), dma((4,)), dma((3,)), dma((3,)),
            pltpu.SemaphoreType.REGULAR,
            dma, dma, dma, dma, dma((3,)), dma((3,)), dma((4,)), dma((4,)),
        ],
        compiler_params=pltpu.CompilerParams(
            collective_id=0, has_side_effects=True, vmem_limit_bytes=60 * 1024 * 1024
        ),
        cost_estimate=pl.CostEstimate(flops=2 * 128 * 16 * FF, bytes_accessed=5_000_000, transcendentals=2 * FF),
        name="compressed_step",
    )(
        hidden[0],
        cotangent[0].T,
        grouped(momentum),
        grouped(worker_error),
        server_error,
        grouped(master),
        grouped(second_moment),
    )

    def rows_of(a):
        return a.transpose(1, 0, 2).reshape(1, 2, FF)

    return rows_of(moment), rows_of(werr), serr, weights


def solution(mesh):
    in_specs = (
        P("dp", "node", None),
        P("dp", "node", None),
        P("dp", "node", None),
        P("dp", "node", None),
        P("node", "dp"),
        P("node", None),
        P("node", None),
    )
    out_specs = (P("dp", "node", None), P("dp", "node", None), P("node", "dp"), P())
    return jax.shard_map(body, mesh=mesh, in_specs=in_specs, out_specs=out_specs, check_vma=False)
```

```python
import functools

import jax
import jax.numpy as jnp
from jax import lax
from jax.experimental import pallas as pl
from jax.experimental.pallas import tpu as pltpu
from jax.sharding import PartitionSpec as P

MESH = pl.DeviceIdType.MESH
F32 = jnp.float32
BF16 = jnp.bfloat16

FF = 13824
LANES = 128
GROUPS = FF // LANES
DENSE = 2 * GROUPS
PADDED = 224
SERVERS = 64
PIECE = FF // SERVERS
QUARTER = GROUPS // 4
BETA = 0.9
EPSILON = 1e-6
RATE = 0.5


def far_first(j, half):
    odd = lax.rem(j, 2)
    return half + (1 - odd) * (j // 2) - odd * ((j + 1) // 2)


def device(x, y, z, c):
    return ((y // 2) * 2 + c, z * 8 + lax.rem(y, 2) * 4 + x)


def kernel(
    hid, cot, mom, werr, serr, mast, second,
    moment_out, werr_out, serr_out, weights_out,
    hid_v, part, core_in, y_out, y_in, mom_v, werr_v, mast_v, second_v, serr_v,
    sent_v, pieces, arrived, wpiece, gathered, wall, spread,
    load_sem, store_sem, core_send, core_recv, y_send, y_recv, ready,
    b_send, b_recv, c_send, c_recv, x_send, x_recv, s_send, s_recv,
):
    node = lax.axis_index("node")
    dp = lax.axis_index("dp")
    c = lax.rem(node, 2)
    yh = node // 2
    z = dp // 8
    yl = lax.rem(dp // 4, 2)
    x = lax.rem(dp, 4)
    y = yh * 2 + yl
    sibling = (node + 1 - 2 * c, dp)

    loads = [
        pltpu.make_async_copy(
            hid.at[:, pl.ds(j * QUARTER * LANES, QUARTER * LANES)],
            hid_v.at[:, pl.ds(j * QUARTER * LANES, QUARTER * LANES)],
            load_sem.at[j],
        )
        for j in range(4)
    ]
    states = [
        pltpu.make_async_copy(mom.reshape(DENSE, LANES), mom_v.at[pl.ds(0, DENSE)], load_sem.at[4]),
        pltpu.make_async_copy(werr.reshape(DENSE, LANES), werr_v.at[pl.ds(0, DENSE)], load_sem.at[5]),
        pltpu.make_async_copy(mast, mast_v.at[pl.ds(0, GROUPS)], load_sem.at[6]),
        pltpu.make_async_copy(second, second_v.at[pl.ds(0, GROUPS)], load_sem.at[7]),
    ]
    for load in loads:
        load.start()

    barrier = pltpu.get_barrier_semaphore()

    def greet(who):
        pl.semaphore_signal(barrier, 1, device_id=who, device_id_type=MESH)

    @pl.loop(0, 7)
    def _(j):
        greet(device(x, y, lax.rem(z + far_first(j, 4), 8), c))
        greet(device(x, lax.rem(y + far_first(j, 4), 8), z, c))

    @pl.loop(1, 4)
    def _(j):
        other = lax.rem(x + j, 4)
        greet(device(other, y, z, c))
        greet(device(other, yh * 2 + 1 - yl, z, c))

    greet(sibling)

    for state in states:
        state.start()

    tail = jnp.zeros((PADDED - DENSE, LANES), F32)
    for a in range(2):
        for b in range(4):
            part[a, b, pl.ds(DENSE, PADDED - DENSE), :] = tail
    mom_v[pl.ds(DENSE, PADDED - DENSE), :] = tail
    werr_v[pl.ds(DENSE, PADDED - DENSE), :] = tail
    mast_v[pl.ds(GROUPS, 4)] = jnp.zeros((4, 2, LANES), F32)
    second_v[pl.ds(GROUPS, 4)] = jnp.zeros((4, 2, LANES), F32)
    serr_v[...] = jnp.zeros((4, LANES), F32)
    serr_v[pl.ds(0, 2), :] = serr[:, pl.ds(0, LANES)]
    serr_v[pl.ds(2, 2), pl.ds(0, PIECE - LANES)] = serr[:, pl.ds(LANES, PIECE - LANES)]

    cot_value = cot[...]
    for j in range(4):
        loads[j].wait()
        sums = jnp.dot(
            cot_value,
            hid_v[:, pl.ds(j * QUARTER * LANES, QUARTER * LANES)],
            preferred_element_type=F32,
        )
        for g in range(QUARTER):
            row = 2 * (j * QUARTER + g)
            for n in range(8):
                part[n % 2, n // 2, pl.ds(row, 2), :] = sums[
                    2 * n : 2 * n + 2, g * LANES : (g + 1) * LANES
                ]

    pl.semaphore_wait(barrier, 21)

    def to_core(d):
        return pltpu.make_async_remote_copy(
            part.at[1 - c, lax.rem(yh + d, 4)], core_in.at[d], core_send.at[d], core_recv.at[d],
            device_id=sibling, device_id_type=MESH,
        )

    def to_node(d):
        return pltpu.make_async_remote_copy(
            y_out.at[d - 1], y_in.at[d - 1], y_send.at[d - 1], y_recv.at[d - 1],
            device_id=(lax.rem(yh + d, 4) * 2 + c, dp), device_id_type=MESH,
        )

    for d in (2, 1, 3, 0):
        to_core(d).start()

    @pl.loop(0, 7)
    def _(j):
        pl.semaphore_signal(
            ready, 1, device_id=device(x, y, lax.rem(z + far_first(j, 4), 8), c), device_id_type=MESH
        )

    for d in (2, 1, 3):
        to_core(d).wait_recv()
        y_out[d - 1] = (part[c, lax.rem(yh + d, 4)] + core_in[d]).astype(BF16)
        to_node(d).start()
    to_core(0).wait_recv()
    gradient = part[c, yh] + core_in[0]
    states[0].wait()
    states[1].wait()
    for d in (1, 3, 2):
        to_node(d).wait_recv()
        gradient = gradient + y_in[d - 1].astype(F32)

    moment = BETA * mom_v[...] + (1.0 - BETA) * gradient
    carried = moment + werr_v[...]
    mom_v[...] = moment
    square = jnp.sum(carried * carried, axis=(0, 1), keepdims=True)
    scale = jnp.sqrt(square / (2 * FF) + EPSILON)
    sent = (scale * jnp.tanh(carried / scale)).astype(BF16).astype(F32)
    sent_v[...] = sent
    werr_v[...] = carried - sent

    lane = lax.broadcasted_iota(jnp.int32, (8, LANES), 1)
    for p in range(SERVERS):
        group, shift = divmod(PIECE * p, LANES)
        rows = sent_v[pl.ds(2 * group, 8), :]
        if shift:
            first = pltpu.roll(rows, LANES - shift, 1)
            rows = jnp.where(lane < LANES - shift, first, pltpu.roll(first, 6, 0))
        pieces[p] = rows[0:4]

    pl.semaphore_wait(ready, 7)

    def to_server(k):
        jz, jx, jy = k // 8, lax.rem(k, 8) // 2, lax.rem(k, 2)
        tz = lax.rem(z + far_first(jz, 4), 8)
        tx = lax.rem(x + far_first(jx, 2), 4)
        ty = lax.rem(yl + 1 - jy, 2)
        target = tz * 8 + ty * 4 + tx
        return pltpu.make_async_remote_copy(
            pieces.at[target], arrived.at[dp], b_send, b_recv, device_id=(node, target), device_id_type=MESH
        )

    @pl.loop(0, SERVERS - 1)
    def _(k):
        to_server(k).start()

    arrived[dp] = pieces[dp]
    moment_store = pltpu.make_async_copy(mom_v.at[pl.ds(0, DENSE)], moment_out.reshape(DENSE, LANES), store_sem.at[0])
    werr_store = pltpu.make_async_copy(werr_v.at[pl.ds(0, DENSE)], werr_out.reshape(DENSE, LANES), store_sem.at[1])
    moment_store.start()
    werr_store.start()

    states[2].wait()
    states[3].wait()
    column = dp * PIECE
    group, shift = column // LANES, lax.rem(column, LANES)

    def own_piece(ref):
        rows = jnp.concatenate([ref[group + j] for j in range(4)], axis=0)
        first = pltpu.roll(rows, lax.rem(LANES - shift, LANES), 1)
        return jnp.where(lane < LANES - shift, first, pltpu.roll(first, 6, 0))[0:4]

    row4 = lax.broadcasted_iota(jnp.int32, (4, LANES), 0)
    lane4 = lax.broadcasted_iota(jnp.int32, (4, LANES), 1)
    valid = (row4 < 2) | (lane4 < PIECE - LANES)
    own_master = own_piece(mast_v)
    divisor = jnp.sqrt(jnp.where(valid, own_piece(second_v), 1.0)) + 1e-8

    everyone = SERVERS - 1
    pltpu.make_async_copy(pieces.at[pl.ds(0, everyone)], arrived.at[pl.ds(0, everyone)], b_recv).wait()
    served = jnp.sum(arrived[...], axis=0) / SERVERS + serr_v[...]
    served = jnp.where(valid, served, 0.0)
    square = jnp.sum(served * served, axis=(0, 1), keepdims=True)
    scale = jnp.sqrt(square / (2 * PIECE) + EPSILON)
    returned = (scale * jnp.tanh(served / scale)).astype(BF16).astype(F32)
    updated = own_master - RATE * (returned / divisor)
    updated = jnp.concatenate([updated[0:1], updated[2:3], updated[1:2], updated[3:4]], axis=0)
    wpiece[...] = updated.astype(BF16).astype(F32)

    slot = (z * 2 + yl) * 4 + yh

    def to_plane(k):
        tz = lax.rem(z + far_first(k // 8, 4), 8)
        ty = lax.rem(y + far_first(lax.rem(k, 8), 4), 8)
        return pltpu.make_async_remote_copy(
            wpiece, gathered.at[slot], c_send, c_recv, device_id=device(x, ty, tz, c), device_id_type=MESH
        )

    @pl.loop(0, SERVERS - 1)
    def _(k):
        to_plane(k).start()

    gathered[slot] = wpiece[...]
    residual = served - returned
    serr_out[:, pl.ds(0, LANES)] = residual[0:2]
    serr_out[:, pl.ds(LANES, PIECE - LANES)] = residual[2:4, 0 : PIECE - LANES]

    pltpu.make_async_copy(pieces.at[pl.ds(0, everyone)], gathered.at[pl.ds(0, everyone)], c_recv).wait()
    wall[c, x] = gathered[...].reshape(4 * SERVERS, LANES).astype(BF16)

    def to_x(d):
        return pltpu.make_async_remote_copy(
            wall.at[c, x], wall.at[c, x], x_send.at[d - 1], x_recv.at[d - 1],
            device_id=(node, dp - x + lax.rem(x + d, 4)), device_id_type=MESH,
        )

    def from_x(d):
        block = wall.at[c, lax.rem(x + 4 - d, 4)]
        return pltpu.make_async_remote_copy(
            block, block, x_send.at[d - 1], x_recv.at[d - 1],
            device_id=(node, dp - x + lax.rem(x + d, 4)), device_id_type=MESH,
        )

    def to_sibling(d):
        block = wall.at[c, lax.rem(x + 4 - d, 4)]
        return pltpu.make_async_remote_copy(
            block, block, s_send.at[d], s_recv.at[d], device_id=sibling, device_id_type=MESH
        )

    def from_sibling(d):
        block = wall.at[1 - c, lax.rem(x + 4 - d, 4)]
        return pltpu.make_async_remote_copy(
            block, block, s_send.at[d], s_recv.at[d], device_id=sibling, device_id_type=MESH
        )

    for d in (2, 1, 3):
        to_x(d).start()
    to_sibling(0).start()
    for d in (1, 3, 2):
        from_x(d).wait_recv()
        to_sibling(d).start()
    for d in (0, 1, 3, 2):
        from_sibling(d).wait_recv()

    @pl.loop(0, 4)
    def _(q):
        parts = [[] for _ in range(QUARTER)]
        for pp in range(16):
            for core in range(2):
                block = wall[core, pp % 4, pl.ds(pl.multiple_of(q * 64 + 16 * (pp // 4), 16), 16), :].astype(F32)
                for h in range(4):
                    spread[pp, pl.ds(8 * h + 4 * core, 4), :] = block[4 * h : 4 * h + 4]
            for half in range(2):
                rows = [spread[pp, pl.ds(16 * h + half, 8, stride=2), :] for h in range(2)]
                begin = PIECE * pp + LANES * half
                end = min(begin + LANES, PIECE * (pp + 1))
                group, shift = divmod(begin, LANES)
                if shift:
                    rows = [pltpu.roll(r, shift, 1) for r in rows]
                for g in (group, group + 1):
                    if max(begin, g * LANES) < min(end, (g + 1) * LANES):
                        parts[g].append((max(begin, g * LANES) - g * LANES, rows))
        for g in range(QUARTER):
            total = parts[g][0][1]
            for low, rows in parts[g][1:]:
                total = [jnp.where(lane < low, t, r) for t, r in zip(total, rows)]
            weights_out[:, pl.ds(pl.multiple_of(q * QUARTER * LANES + g * LANES, LANES), LANES)] = (
                jnp.concatenate(total, axis=0).astype(BF16)
            )

    moment_store.wait()
    werr_store.wait()
    for d in range(4):
        to_core(d).wait_send()
        to_sibling(d).wait_send()
    for d in range(1, 4):
        to_node(d).wait_send()
        to_x(d).wait_send()
    pltpu.make_async_copy(pieces.at[pl.ds(0, everyone)], arrived.at[pl.ds(0, everyone)], b_send).wait()
    pltpu.make_async_copy(pieces.at[pl.ds(0, everyone)], gathered.at[pl.ds(0, everyone)], c_send).wait()


def finish(*refs):
    sems = refs[8]
    copies = [pltpu.make_async_copy(refs[i], refs[4 + i], sems.at[i]) for i in (3, 0, 1, 2)]
    for copy in copies:
        copy.start()
    for copy in copies:
        copy.wait()


def grouped(a):
    return a.reshape(2, GROUPS, LANES).transpose(1, 0, 2)


def body(hidden, cotangent, momentum, worker_error, server_error, master, second_moment):
    anywhere = pl.BlockSpec(memory_space=pl.ANY)
    vmem = pl.BlockSpec(memory_space=pltpu.VMEM)
    dma = pltpu.SemaphoreType.DMA
    moment, werr, serr, weights = pl.pallas_call(
        kernel,
        out_shape=[
            pltpu.VMEM((GROUPS, 2, LANES), F32),
            pltpu.VMEM((GROUPS, 2, LANES), F32),
            pltpu.VMEM((2, PIECE), F32),
            pltpu.VMEM((16, FF), BF16),
        ],
        in_specs=[anywhere, vmem, anywhere, anywhere, vmem, anywhere, anywhere],
        out_specs=[anywhere, anywhere, vmem, vmem],
        scratch_shapes=[
            pltpu.VMEM((128, FF), BF16),
            pltpu.VMEM((2, 4, PADDED, LANES), F32),
            pltpu.VMEM((4, PADDED, LANES), F32),
            pltpu.VMEM((3, PADDED, LANES), BF16),
            pltpu.VMEM((3, PADDED, LANES), BF16),
            pltpu.VMEM((PADDED, LANES), F32),
            pltpu.VMEM((PADDED, LANES), F32),
            pltpu.VMEM((GROUPS + 4, 2, LANES), F32),
            pltpu.VMEM((GROUPS + 4, 2, LANES), F32),
            pltpu.VMEM((4, LANES), F32),
            pltpu.VMEM((PADDED, LANES), F32),
            pltpu.VMEM((SERVERS, 4, LANES), F32),
            pltpu.VMEM((SERVERS, 4, LANES), F32),
            pltpu.VMEM((4, LANES), F32),
            pltpu.VMEM((SERVERS, 4, LANES), F32),
            pltpu.VMEM((2, 4, 4 * SERVERS, LANES), BF16),
            pltpu.VMEM((16, 32, LANES), F32),
            dma((8,)), dma((2,)), dma((4,)), dma((4,)), dma((3,)), dma((3,)),
            pltpu.SemaphoreType.REGULAR,
            dma, dma, dma, dma, dma((3,)), dma((3,)), dma((4,)), dma((4,)),
        ],
        compiler_params=pltpu.CompilerParams(
            collective_id=0, has_side_effects=True, vmem_limit_bytes=60 * 1024 * 1024
        ),
        cost_estimate=pl.CostEstimate(flops=2 * 128 * 16 * FF, bytes_accessed=5_000_000, transcendentals=2 * FF),
        name="compressed_step",
    )(
        hidden[0],
        cotangent[0].T,
        grouped(momentum),
        grouped(worker_error),
        server_error,
        grouped(master),
        grouped(second_moment),
    )

    moment, werr, serr, weights = pl.pallas_call(
        finish,
        out_shape=[jax.ShapeDtypeStruct(a.shape, a.dtype) for a in (moment, werr, serr, weights)],
        in_specs=[anywhere] * 4,
        out_specs=[anywhere] * 4,
        scratch_shapes=[dma((4,))],
        compiler_params=pltpu.CompilerParams(vmem_limit_bytes=1024 * 1024),
        name="finish",
    )(moment, werr, serr, weights)

    def rows_of(a):
        return a.transpose(1, 0, 2).reshape(1, 2, FF)

    return rows_of(moment), rows_of(werr), serr, weights


def solution(mesh):
    in_specs = (
        P("dp", "node", None),
        P("dp", "node", None),
        P("dp", "node", None),
        P("dp", "node", None),
        P("node", "dp"),
        P("node", None),
        P("node", None),
    )
    out_specs = (P("dp", "node", None), P("dp", "node", None), P("node", "dp"), P())
    return jax.shard_map(body, mesh=mesh, in_specs=in_specs, out_specs=out_specs, check_vma=False)
```

```python
import functools

import jax
import jax.numpy as jnp
from jax import lax
from jax.experimental import pallas as pl
from jax.experimental.pallas import tpu as pltpu
from jax.sharding import PartitionSpec as P

MESH = pl.DeviceIdType.MESH
F32 = jnp.float32
BF16 = jnp.bfloat16

FF = 13824
LANES = 128
GROUPS = FF // LANES
DENSE = 2 * GROUPS
PADDED = 224
SERVERS = 64
PIECE = FF // SERVERS
QUARTER = GROUPS // 4
BETA = 0.9
EPSILON = 1e-6
RATE = 0.5


def far_first(j, half):
    odd = lax.rem(j, 2)
    return half + (1 - odd) * (j // 2) - odd * ((j + 1) // 2)


def device(x, y, z, c):
    return ((y // 2) * 2 + c, z * 8 + lax.rem(y, 2) * 4 + x)


def kernel(
    hid, cot, mom, werr, serr, mast, second,
    moment_out, werr_out, serr_out, weights_out,
    hid_v, part, core_in, y_out, y_in, mom_v, werr_v, mast_v, second_v, serr_v,
    sent_v, pieces, arrived, wpiece, wall, spread,
    load_sem, store_sem, core_send, core_recv, y_send, y_recv, ready,
    b_send, b_recv, c_send, c_recv, x_send, x_recv, s_send, s_recv,
):
    node = lax.axis_index("node")
    dp = lax.axis_index("dp")
    c = lax.rem(node, 2)
    yh = node // 2
    z = dp // 8
    yl = lax.rem(dp // 4, 2)
    x = lax.rem(dp, 4)
    y = yh * 2 + yl
    sibling = (node + 1 - 2 * c, dp)

    loads = [
        pltpu.make_async_copy(
            hid.at[:, pl.ds(j * QUARTER * LANES, QUARTER * LANES)],
            hid_v.at[:, pl.ds(j * QUARTER * LANES, QUARTER * LANES)],
            load_sem.at[j],
        )
        for j in range(4)
    ]
    states = [
        pltpu.make_async_copy(mom.reshape(DENSE, LANES), mom_v.at[pl.ds(0, DENSE)], load_sem.at[4]),
        pltpu.make_async_copy(werr.reshape(DENSE, LANES), werr_v.at[pl.ds(0, DENSE)], load_sem.at[5]),
        pltpu.make_async_copy(mast, mast_v.at[pl.ds(0, GROUPS)], load_sem.at[6]),
        pltpu.make_async_copy(second, second_v.at[pl.ds(0, GROUPS)], load_sem.at[7]),
    ]
    for load in loads:
        load.start()

    barrier = pltpu.get_barrier_semaphore()

    def greet(who):
        pl.semaphore_signal(barrier, 1, device_id=who, device_id_type=MESH)

    @pl.loop(0, 7)
    def _(j):
        greet(device(x, y, lax.rem(z + far_first(j, 4), 8), c))
        greet(device(x, lax.rem(y + far_first(j, 4), 8), z, c))

    @pl.loop(1, 4)
    def _(j):
        other = lax.rem(x + j, 4)
        greet(device(other, y, z, c))
        greet(device(other, yh * 2 + 1 - yl, z, c))

    greet(sibling)

    for state in states:
        state.start()

    tail = jnp.zeros((PADDED - DENSE, LANES), F32)
    for a in range(2):
        for b in range(4):
            part[a, b, pl.ds(DENSE, PADDED - DENSE), :] = tail
    mom_v[pl.ds(DENSE, PADDED - DENSE), :] = tail
    werr_v[pl.ds(DENSE, PADDED - DENSE), :] = tail
    mast_v[pl.ds(GROUPS, 4)] = jnp.zeros((4, 2, LANES), F32)
    second_v[pl.ds(GROUPS, 4)] = jnp.zeros((4, 2, LANES), F32)
    serr_v[...] = jnp.zeros((4, LANES), F32)
    serr_v[pl.ds(0, 2), :] = serr[:, pl.ds(0, LANES)]
    serr_v[pl.ds(2, 2), pl.ds(0, PIECE - LANES)] = serr[:, pl.ds(LANES, PIECE - LANES)]

    cot_value = cot[...]
    for j in range(4):
        loads[j].wait()
        sums = jnp.dot(
            cot_value,
            hid_v[:, pl.ds(j * QUARTER * LANES, QUARTER * LANES)],
            preferred_element_type=F32,
        )
        for g in range(QUARTER):
            row = 2 * (j * QUARTER + g)
            for n in range(8):
                part[n % 2, n // 2, pl.ds(row, 2), :] = sums[
                    2 * n : 2 * n + 2, g * LANES : (g + 1) * LANES
                ]

    pl.semaphore_wait(barrier, 21)

    def to_core(d):
        return pltpu.make_async_remote_copy(
            part.at[1 - c, lax.rem(yh + d, 4)], core_in.at[d], core_send.at[d], core_recv.at[d],
            device_id=sibling, device_id_type=MESH,
        )

    def to_node(d):
        return pltpu.make_async_remote_copy(
            y_out.at[d - 1], y_in.at[d - 1], y_send.at[d - 1], y_recv.at[d - 1],
            device_id=(lax.rem(yh + d, 4) * 2 + c, dp), device_id_type=MESH,
        )

    for d in (2, 1, 3, 0):
        to_core(d).start()

    @pl.loop(0, 7)
    def _(j):
        pl.semaphore_signal(
            ready, 1, device_id=device(x, y, lax.rem(z + far_first(j, 4), 8), c), device_id_type=MESH
        )

    for d in (2, 1, 3):
        to_core(d).wait_recv()
        y_out[d - 1] = (part[c, lax.rem(yh + d, 4)] + core_in[d]).astype(BF16)
        to_node(d).start()
    to_core(0).wait_recv()
    gradient = part[c, yh] + core_in[0]
    states[0].wait()
    states[1].wait()
    for d in (1, 3, 2):
        to_node(d).wait_recv()
        gradient = gradient + y_in[d - 1].astype(F32)

    moment = BETA * mom_v[...] + (1.0 - BETA) * gradient
    carried = moment + werr_v[...]
    mom_v[...] = moment
    square = jnp.sum(carried * carried, axis=(0, 1), keepdims=True)
    scale = jnp.sqrt(square / (2 * FF) + EPSILON)
    sent = (scale * jnp.tanh(carried * (1.0 / scale))).astype(BF16).astype(F32)
    sent_v[...] = sent
    werr_v[...] = carried - sent

    lane = lax.broadcasted_iota(jnp.int32, (8, LANES), 1)
    for p in range(SERVERS):
        group, shift = divmod(PIECE * p, LANES)
        rows = sent_v[pl.ds(2 * group, 8), :]
        if shift:
            first = pltpu.roll(rows, LANES - shift, 1)
            rows = jnp.where(lane < LANES - shift, first, pltpu.roll(first, 6, 0))
        pieces[p] = rows[0:4].astype(BF16)

    pl.semaphore_wait(ready, 7)

    def to_server(k):
        jz, jx, jy = k // 8, lax.rem(k, 8) // 2, lax.rem(k, 2)
        tz = lax.rem(z + far_first(jz, 4), 8)
        tx = lax.rem(x + far_first(jx, 2), 4)
        ty = lax.rem(yl + 1 - jy, 2)
        target = tz * 8 + ty * 4 + tx
        return pltpu.make_async_remote_copy(
            pieces.at[target], arrived.at[dp], b_send, b_recv, device_id=(node, target), device_id_type=MESH
        )

    @pl.loop(0, SERVERS - 1, unroll=7)
    def _(k):
        to_server(k).start()

    arrived[dp] = pieces[dp]
    moment_store = pltpu.make_async_copy(mom_v.at[pl.ds(0, DENSE)], moment_out.reshape(DENSE, LANES), store_sem.at[0])
    werr_store = pltpu.make_async_copy(werr_v.at[pl.ds(0, DENSE)], werr_out.reshape(DENSE, LANES), store_sem.at[1])
    moment_store.start()
    werr_store.start()

    states[2].wait()
    states[3].wait()
    column = dp * PIECE
    group, shift = column // LANES, lax.rem(column, LANES)

    def own_piece(ref):
        rows = jnp.concatenate([ref[group + j] for j in range(4)], axis=0)
        first = pltpu.roll(rows, lax.rem(LANES - shift, LANES), 1)
        return jnp.where(lane < LANES - shift, first, pltpu.roll(first, 6, 0))[0:4]

    row4 = lax.broadcasted_iota(jnp.int32, (4, LANES), 0)
    lane4 = lax.broadcasted_iota(jnp.int32, (4, LANES), 1)
    valid = (row4 < 2) | (lane4 < PIECE - LANES)
    own_master = own_piece(mast_v)
    step = RATE / (jnp.sqrt(jnp.where(valid, own_piece(second_v), 1.0)) + 1e-8)

    others = pl.ds(0, SERVERS - 1)
    pltpu.make_async_copy(arrived.at[others], arrived.at[others], b_recv).wait()
    served = jnp.sum(arrived[...].astype(F32), axis=0) / SERVERS + serr_v[...]
    served = jnp.where(valid, served, 0.0)
    square = jnp.sum(served * served, axis=(0, 1), keepdims=True)
    scale = jnp.sqrt(square / (2 * PIECE) + EPSILON)
    returned = (scale * jnp.tanh(served / scale)).astype(BF16).astype(F32)
    updated = own_master - step * returned
    updated = jnp.concatenate([updated[0:1], updated[2:3], updated[1:2], updated[3:4]], axis=0)
    wpiece[...] = updated.astype(BF16)

    slot = yl * 4 + yh

    def to_plane(k):
        dz = far_first(k // 8, 4)
        ty = lax.rem(y + far_first(lax.rem(k, 8), 4), 8)
        return pltpu.make_async_remote_copy(
            wpiece, wall.at[c, x, z, slot], c_send, c_recv.at[dz],
            device_id=device(x, ty, lax.rem(z + dz, 8), c), device_id_type=MESH,
        )

    @pl.loop(0, SERVERS - 1, unroll=7)
    def _(k):
        to_plane(k).start()

    wall[c, x, z, slot] = wpiece[...]
    residual = served - returned
    serr_out[:, pl.ds(0, LANES)] = residual[0:2]
    serr_out[:, pl.ds(LANES, PIECE - LANES)] = residual[2:4, 0 : PIECE - LANES]

    def to_x(d, source):
        block = wall.at[c, x, source]
        return pltpu.make_async_remote_copy(
            block, block, x_send, x_recv.at[d - 1],
            device_id=(node, dp - x + lax.rem(x + d, 4)), device_id_type=MESH,
        )

    def to_sibling(block):
        return pltpu.make_async_remote_copy(
            block, block, s_send, s_recv, device_id=sibling, device_id_type=MESH
        )

    for dz in (0, 1, 7, 2, 6, 3, 5, 4):
        source = lax.rem(z + 8 - dz, 8)
        landed = wall.at[c, x, source, pl.ds(0, 8 if dz else 7)]
        pltpu.make_async_copy(landed, landed, c_recv.at[dz]).wait()
        for d in (2, 1, 3):
            to_x(d, source).start()
        to_sibling(wall.at[c, x, source]).start()
    for d in (1, 3, 2):
        block = wall.at[c, lax.rem(x + 4 - d, 4)]
        pltpu.make_async_copy(block, block, x_recv.at[d - 1]).wait()
        to_sibling(block).start()
    pltpu.make_async_copy(wall.at[1 - c], wall.at[1 - c], s_recv).wait()

    @pl.loop(0, 4)
    def _(q):
        parts = [[] for _ in range(QUARTER)]
        for pp in range(16):
            for core in range(2):
                for h in range(4):
                    spread[pp, pl.ds(8 * h + 4 * core, 4), :] = wall[
                        core, pp % 4, 2 * q + pp // 8, pp // 4 % 2 * 4 + h
                    ].astype(F32)
            for half in range(2):
                rows = [spread[pp, pl.ds(16 * h + half, 8, stride=2), :] for h in range(2)]
                begin = PIECE * pp + LANES * half
                end = min(begin + LANES, PIECE * (pp + 1))
                group, shift = divmod(begin, LANES)
                if shift:
                    rows = [pltpu.roll(r, shift, 1) for r in rows]
                for g in (group, group + 1):
                    if max(begin, g * LANES) < min(end, (g + 1) * LANES):
                        parts[g].append((max(begin, g * LANES) - g * LANES, rows))
        for g in range(QUARTER):
            total = parts[g][0][1]
            for low, rows in parts[g][1:]:
                total = [jnp.where(lane < low, t, r) for t, r in zip(total, rows)]
            weights_out[:, pl.ds(pl.multiple_of(q * QUARTER * LANES + g * LANES, LANES), LANES)] = (
                jnp.concatenate(total, axis=0).astype(BF16)
            )

    moment_store.wait()
    werr_store.wait()
    for d in range(4):
        to_core(d).wait_send()
    for d in range(1, 4):
        to_node(d).wait_send()
    pltpu.make_async_copy(arrived.at[others], arrived.at[others], b_send).wait()
    pltpu.make_async_copy(arrived.at[others], arrived.at[others], c_send).wait()
    pltpu.make_async_copy(wall.at[c, pl.ds(0, 3)], wall.at[c, pl.ds(0, 3)], x_send).wait()
    pltpu.make_async_copy(wall.at[c], wall.at[c], s_send).wait()


def finish(*refs):
    sems = refs[8]
    copies = [pltpu.make_async_copy(refs[i], refs[4 + i], sems.at[i]) for i in (3, 0, 1, 2)]
    for copy in copies:
        copy.start()
    for copy in copies:
        copy.wait()


def grouped(a):
    return a.reshape(2, GROUPS, LANES).transpose(1, 0, 2)


def body(hidden, cotangent, momentum, worker_error, server_error, master, second_moment):
    anywhere = pl.BlockSpec(memory_space=pl.ANY)
    vmem = pl.BlockSpec(memory_space=pltpu.VMEM)
    dma = pltpu.SemaphoreType.DMA
    moment, werr, serr, weights = pl.pallas_call(
        kernel,
        out_shape=[
            pltpu.VMEM((GROUPS, 2, LANES), F32),
            pltpu.VMEM((GROUPS, 2, LANES), F32),
            pltpu.VMEM((2, PIECE), F32),
            pltpu.VMEM((16, FF), BF16),
        ],
        in_specs=[anywhere, vmem, anywhere, anywhere, vmem, anywhere, anywhere],
        out_specs=[anywhere, anywhere, vmem, vmem],
        scratch_shapes=[
            pltpu.VMEM((128, FF), BF16),
            pltpu.VMEM((2, 4, PADDED, LANES), F32),
            pltpu.VMEM((4, PADDED, LANES), F32),
            pltpu.VMEM((3, PADDED, LANES), BF16),
            pltpu.VMEM((3, PADDED, LANES), BF16),
            pltpu.VMEM((PADDED, LANES), F32),
            pltpu.VMEM((PADDED, LANES), F32),
            pltpu.VMEM((GROUPS + 4, 2, LANES), F32),
            pltpu.VMEM((GROUPS + 4, 2, LANES), F32),
            pltpu.VMEM((4, LANES), F32),
            pltpu.VMEM((PADDED, LANES), F32),
            pltpu.VMEM((SERVERS, 4, LANES), BF16),
            pltpu.VMEM((SERVERS, 4, LANES), BF16),
            pltpu.VMEM((4, LANES), BF16),
            pltpu.VMEM((2, 4, 8, 8, 4, LANES), BF16),
            pltpu.VMEM((16, 32, LANES), F32),
            dma((8,)), dma((2,)), dma((4,)), dma((4,)), dma((3,)), dma((3,)),
            pltpu.SemaphoreType.REGULAR,
            dma, dma, dma, dma((8,)), dma, dma((3,)), dma, dma,
        ],
        compiler_params=pltpu.CompilerParams(
            collective_id=0, has_side_effects=True, vmem_limit_bytes=60 * 1024 * 1024
        ),
        cost_estimate=pl.CostEstimate(flops=2 * 128 * 16 * FF, bytes_accessed=5_000_000, transcendentals=2 * FF),
        name="compressed_step",
    )(
        hidden[0],
        cotangent[0].T,
        grouped(momentum),
        grouped(worker_error),
        server_error,
        grouped(master),
        grouped(second_moment),
    )

    moment, werr, serr, weights = pl.pallas_call(
        finish,
        out_shape=[jax.ShapeDtypeStruct(a.shape, a.dtype) for a in (moment, werr, serr, weights)],
        in_specs=[anywhere] * 4,
        out_specs=[anywhere] * 4,
        scratch_shapes=[dma((4,))],
        compiler_params=pltpu.CompilerParams(vmem_limit_bytes=1024 * 1024),
        name="finish",
    )(moment, werr, serr, weights)

    def rows_of(a):
        return a.transpose(1, 0, 2).reshape(1, 2, FF)

    return rows_of(moment), rows_of(werr), serr, weights


def solution(mesh):
    in_specs = (
        P("dp", "node", None),
        P("dp", "node", None),
        P("dp", "node", None),
        P("dp", "node", None),
        P("node", "dp"),
        P("node", None),
        P("node", None),
    )
    out_specs = (P("dp", "node", None), P("dp", "node", None), P("node", "dp"), P())
    return jax.shard_map(body, mesh=mesh, in_specs=in_specs, out_specs=out_specs, check_vma=False)
```

```python
import functools

import jax
import jax.numpy as jnp
from jax import lax
from jax.experimental import pallas as pl
from jax.experimental.pallas import tpu as pltpu
from jax.sharding import PartitionSpec as P

MESH = pl.DeviceIdType.MESH
F32 = jnp.float32
BF16 = jnp.bfloat16

FF = 13824
LANES = 128
GROUPS = FF // LANES
DENSE = 2 * GROUPS
PADDED = 224
SERVERS = 64
PIECE = FF // SERVERS
QUARTER = GROUPS // 4
BETA = 0.9
EPSILON = 1e-6
RATE = 0.5


def far_first(j, half):
    odd = lax.rem(j, 2)
    return half + (1 - odd) * (j // 2) - odd * ((j + 1) // 2)


def device(x, y, z, c):
    return ((y // 2) * 2 + c, z * 8 + lax.rem(y, 2) * 4 + x)


def kernel(
    hid, cot, mom, werr, serr, mast, second,
    moment_out, werr_out, serr_out, weights_out,
    cot_v, serr_raw, hid_v, part, core_out, core_in, y_out, y_in, mom_v, werr_v, mast_v, second_v, serr_v,
    sent_v, pieces, arrived, wpiece, wall, spread,
    load_sem, store_sem, core_send, core_recv, y_send, y_recv, ready,
    b_send, b_recv, c_send, c_recv, x_send, x_recv, s_send, s_recv,
):
    node = lax.axis_index("node")
    dp = lax.axis_index("dp")
    c = lax.rem(node, 2)
    yh = node // 2
    z = dp // 8
    yl = lax.rem(dp // 4, 2)
    x = lax.rem(dp, 4)
    y = yh * 2 + yl
    sibling = (node + 1 - 2 * c, dp)

    loads = [
        pltpu.make_async_copy(
            hid.at[:, pl.ds(j * QUARTER * LANES, QUARTER * LANES)],
            hid_v.at[:, pl.ds(j * QUARTER * LANES, QUARTER * LANES)],
            load_sem.at[j],
        )
        for j in range(4)
    ]
    states = [
        pltpu.make_async_copy(mom.reshape(DENSE, LANES), mom_v.at[pl.ds(0, DENSE)], load_sem.at[4]),
        pltpu.make_async_copy(werr.reshape(DENSE, LANES), werr_v.at[pl.ds(0, DENSE)], load_sem.at[5]),
        pltpu.make_async_copy(mast, mast_v.at[pl.ds(0, GROUPS)], load_sem.at[6]),
        pltpu.make_async_copy(second, second_v.at[pl.ds(0, GROUPS)], load_sem.at[7]),
        pltpu.make_async_copy(serr, serr_raw, load_sem.at[8]),
    ]
    barrier = pltpu.get_barrier_semaphore()

    def greet(who):
        pl.semaphore_signal(barrier, 1, device_id=who, device_id_type=MESH)

    for d in (4, 2, 6):
        greet(device(x, lax.rem(y + d, 8), z, c))
    greet(sibling)
    cot_load = pltpu.make_async_copy(cot, cot_v, load_sem.at[9])
    cot_load.start()
    for load in loads:
        load.start()
    for d in (4, 3, 5, 2, 6, 1, 7):
        greet(device(x, y, lax.rem(z + d, 8), c))
    for d in (3, 5, 1, 7):
        greet(device(x, lax.rem(y + d, 8), z, c))
    for d in (2, 1, 3):
        greet(device(lax.rem(x + d, 4), yh * 2 + 1 - yl, z, c))
        greet(device(lax.rem(x + d, 4), y, z, c))

    for state in states:
        state.start()

    tail = jnp.zeros((PADDED - DENSE, LANES), F32)
    for a in range(2):
        for b in range(4):
            part[a, b, pl.ds(DENSE, PADDED - DENSE), :] = tail
    mom_v[pl.ds(DENSE, PADDED - DENSE), :] = tail
    werr_v[pl.ds(DENSE, PADDED - DENSE), :] = tail
    mast_v[pl.ds(GROUPS, 4)] = jnp.zeros((4, 2, LANES), F32)
    second_v[pl.ds(GROUPS, 4)] = jnp.zeros((4, 2, LANES), F32)
    serr_v[...] = jnp.zeros((4, LANES), F32)

    cot_load.wait()
    cot_value = cot_v[...]
    for j in range(4):
        loads[j].wait()
        sums = jnp.dot(
            cot_value,
            hid_v[:, pl.ds(j * QUARTER * LANES, QUARTER * LANES)],
            preferred_element_type=F32,
        )
        for g in range(QUARTER):
            row = 2 * (j * QUARTER + g)
            for n in range(8):
                part[n % 2, n // 2, pl.ds(row, 2), :] = sums[
                    2 * n : 2 * n + 2, g * LANES : (g + 1) * LANES
                ]

    for d in range(4):
        core_out[d] = part[1 - c, lax.rem(yh + d, 4)].astype(BF16)
    pl.semaphore_wait(barrier, 21)

    def to_core(d):
        return pltpu.make_async_remote_copy(
            core_out.at[d], core_in.at[d], core_send.at[d], core_recv.at[d],
            device_id=sibling, device_id_type=MESH,
        )

    def to_node(d):
        return pltpu.make_async_remote_copy(
            y_out.at[d - 1], y_in.at[d - 1], y_send.at[d - 1], y_recv.at[d - 1],
            device_id=(lax.rem(yh + d, 4) * 2 + c, dp), device_id_type=MESH,
        )

    for d in (2, 1, 3, 0):
        to_core(d).start()

    for d in (2, 1, 3):
        to_core(d).wait_recv()
        y_out[d - 1] = (part[c, lax.rem(yh + d, 4)] + core_in[d].astype(F32)).astype(BF16)
        to_node(d).start()
    for d in (4, 3, 5, 2, 6, 1, 7):
        pl.semaphore_signal(
            ready, 1, device_id=device(x, y, lax.rem(z + d, 8), c), device_id_type=MESH
        )
    to_core(0).wait_recv()
    gradient = part[c, yh] + core_in[0].astype(F32)
    states[0].wait()
    states[1].wait()
    for d in (1, 3, 2):
        to_node(d).wait_recv()
        gradient = gradient + y_in[d - 1].astype(F32)

    moment = BETA * mom_v[...] + (1.0 - BETA) * gradient
    carried = moment + werr_v[...]
    mom_v[...] = moment
    square = jnp.sum(carried * carried, axis=(0, 1), keepdims=True)
    scale = jnp.sqrt(square / (2 * FF) + EPSILON)
    sent = (scale * jnp.tanh(carried * (1.0 / scale))).astype(BF16).astype(F32)
    sent_v[...] = sent
    werr_v[...] = carried - sent

    lane = lax.broadcasted_iota(jnp.int32, (8, LANES), 1)
    for p in range(SERVERS):
        group, shift = divmod(PIECE * p, LANES)
        rows = sent_v[pl.ds(2 * group, 8), :]
        if shift:
            first = pltpu.roll(rows, LANES - shift, 1)
            rows = jnp.where(lane < LANES - shift, first, pltpu.roll(first, 6, 0))
        pieces[p] = rows[0:4].astype(BF16)

    pl.semaphore_wait(ready, 7)

    def to_server(k):
        jz, jx, jy = k // 8, lax.rem(k, 8) // 2, lax.rem(k, 2)
        tz = lax.rem(z + far_first(jz, 4), 8)
        tx = lax.rem(x + far_first(jx, 2), 4)
        ty = lax.rem(yl + 1 - jy, 2)
        target = tz * 8 + ty * 4 + tx
        return pltpu.make_async_remote_copy(
            pieces.at[target], arrived.at[dp], b_send, b_recv, device_id=(node, target), device_id_type=MESH
        )

    @pl.loop(0, SERVERS - 1, unroll=7)
    def _(k):
        to_server(k).start()

    arrived[dp] = pieces[dp]
    moment_store = pltpu.make_async_copy(mom_v.at[pl.ds(0, DENSE)], moment_out.reshape(DENSE, LANES), store_sem.at[0])
    werr_store = pltpu.make_async_copy(werr_v.at[pl.ds(0, DENSE)], werr_out.reshape(DENSE, LANES), store_sem.at[1])
    moment_store.start()
    werr_store.start()

    states[2].wait()
    states[3].wait()
    states[4].wait()
    serr_v[pl.ds(0, 2), :] = serr_raw[:, pl.ds(0, LANES)]
    serr_v[pl.ds(2, 2), pl.ds(0, PIECE - LANES)] = serr_raw[:, pl.ds(LANES, PIECE - LANES)]
    column = dp * PIECE
    group, shift = column // LANES, lax.rem(column, LANES)

    def own_piece(ref):
        rows = jnp.concatenate([ref[group + j] for j in range(4)], axis=0)
        first = pltpu.roll(rows, lax.rem(LANES - shift, LANES), 1)
        return jnp.where(lane < LANES - shift, first, pltpu.roll(first, 6, 0))[0:4]

    row4 = lax.broadcasted_iota(jnp.int32, (4, LANES), 0)
    lane4 = lax.broadcasted_iota(jnp.int32, (4, LANES), 1)
    valid = (row4 < 2) | (lane4 < PIECE - LANES)
    own_master = own_piece(mast_v)
    step = RATE / (jnp.sqrt(jnp.where(valid, own_piece(second_v), 1.0)) + 1e-8)

    others = pl.ds(0, SERVERS - 1)
    pltpu.make_async_copy(arrived.at[others], arrived.at[others], b_recv).wait()
    served = jnp.sum(arrived[...].astype(F32), axis=0) / SERVERS + serr_v[...]
    served = jnp.where(valid, served, 0.0)
    square = jnp.sum(served * served, axis=(0, 1), keepdims=True)
    scale = jnp.sqrt(square / (2 * PIECE) + EPSILON)
    returned = (scale * jnp.tanh(served / scale)).astype(BF16).astype(F32)
    updated = own_master - step * returned
    updated = jnp.concatenate([updated[0:1], updated[2:3], updated[1:2], updated[3:4]], axis=0)
    wpiece[...] = updated.astype(BF16)

    slot = yl * 4 + yh

    def to_plane(k):
        dz = far_first(k // 8, 4)
        ty = lax.rem(y + far_first(lax.rem(k, 8), 4), 8)
        return pltpu.make_async_remote_copy(
            wpiece, wall.at[c, x, z, slot], c_send, c_recv.at[dz],
            device_id=device(x, ty, lax.rem(z + dz, 8), c), device_id_type=MESH,
        )

    @pl.loop(0, SERVERS - 1, unroll=7)
    def _(k):
        to_plane(k).start()

    wall[c, x, z, slot] = wpiece[...]
    residual = served - returned
    serr_out[:, pl.ds(0, LANES)] = residual[0:2]
    serr_out[:, pl.ds(LANES, PIECE - LANES)] = residual[2:4, 0 : PIECE - LANES]

    def to_x(d, source):
        block = wall.at[c, x, source]
        return pltpu.make_async_remote_copy(
            block, block, x_send, x_recv.at[d - 1],
            device_id=(node, dp - x + lax.rem(x + d, 4)), device_id_type=MESH,
        )

    def to_sibling(block):
        return pltpu.make_async_remote_copy(
            block, block, s_send, s_recv, device_id=sibling, device_id_type=MESH
        )

    for dz in (0, 1, 7, 2, 6, 3, 5, 4):
        source = lax.rem(z + 8 - dz, 8)
        landed = wall.at[c, x, source, pl.ds(0, 8 if dz else 7)]
        pltpu.make_async_copy(landed, landed, c_recv.at[dz]).wait()
        for d in (2, 1, 3):
            to_x(d, source).start()
        to_sibling(wall.at[c, x, source]).start()
    for d in (1, 3, 2):
        block = wall.at[c, lax.rem(x + 4 - d, 4)]
        pltpu.make_async_copy(block, block, x_recv.at[d - 1]).wait()
        to_sibling(block).start()
    pltpu.make_async_copy(wall.at[1 - c], wall.at[1 - c], s_recv).wait()

    @pl.loop(0, 4)
    def _(q):
        parts = [[] for _ in range(QUARTER)]
        for pp in range(16):
            for core in range(2):
                for h in range(4):
                    spread[pp, pl.ds(8 * h + 4 * core, 4), :] = wall[
                        core, pp % 4, 2 * q + pp // 8, pp // 4 % 2 * 4 + h
                    ].astype(F32)
            for half in range(2):
                rows = [spread[pp, pl.ds(16 * h + half, 8, stride=2), :] for h in range(2)]
                begin = PIECE * pp + LANES * half
                end = min(begin + LANES, PIECE * (pp + 1))
                group, shift = divmod(begin, LANES)
                if shift:
                    rows = [pltpu.roll(r, shift, 1) for r in rows]
                for g in (group, group + 1):
                    if max(begin, g * LANES) < min(end, (g + 1) * LANES):
                        parts[g].append((max(begin, g * LANES) - g * LANES, rows))
        for g in range(QUARTER):
            total = parts[g][0][1]
            for low, rows in parts[g][1:]:
                total = [jnp.where(lane < low, t, r) for t, r in zip(total, rows)]
            weights_out[:, pl.ds(pl.multiple_of(q * QUARTER * LANES + g * LANES, LANES), LANES)] = (
                jnp.concatenate(total, axis=0).astype(BF16)
            )

    moment_store.wait()
    werr_store.wait()
    for d in range(4):
        to_core(d).wait_send()
    for d in range(1, 4):
        to_node(d).wait_send()
    pltpu.make_async_copy(arrived.at[others], arrived.at[others], b_send).wait()
    pltpu.make_async_copy(arrived.at[others], arrived.at[others], c_send).wait()
    pltpu.make_async_copy(wall.at[c, pl.ds(0, 3)], wall.at[c, pl.ds(0, 3)], x_send).wait()
    pltpu.make_async_copy(wall.at[c], wall.at[c], s_send).wait()


def finish(*refs):
    sems = refs[8]
    copies = [pltpu.make_async_copy(refs[i], refs[4 + i], sems.at[i]) for i in (3, 0, 1, 2)]
    for copy in copies:
        copy.start()
    for copy in copies:
        copy.wait()


def grouped(a):
    return a.reshape(2, GROUPS, LANES).transpose(1, 0, 2)


def body(hidden, cotangent, momentum, worker_error, server_error, master, second_moment):
    anywhere = pl.BlockSpec(memory_space=pl.ANY)
    vmem = pl.BlockSpec(memory_space=pltpu.VMEM)
    dma = pltpu.SemaphoreType.DMA
    moment, werr, serr, weights = pl.pallas_call(
        kernel,
        out_shape=[
            pltpu.VMEM((GROUPS, 2, LANES), F32),
            pltpu.VMEM((GROUPS, 2, LANES), F32),
            pltpu.VMEM((2, PIECE), F32),
            pltpu.VMEM((16, FF), BF16),
        ],
        in_specs=[anywhere] * 7,
        out_specs=[anywhere, anywhere, vmem, vmem],
        scratch_shapes=[
            pltpu.VMEM((16, 128), BF16),
            pltpu.VMEM((2, PIECE), F32),
            pltpu.VMEM((128, FF), BF16),
            pltpu.VMEM((2, 4, PADDED, LANES), F32),
            pltpu.VMEM((4, PADDED, LANES), BF16),
            pltpu.VMEM((4, PADDED, LANES), BF16),
            pltpu.VMEM((3, PADDED, LANES), BF16),
            pltpu.VMEM((3, PADDED, LANES), BF16),
            pltpu.VMEM((PADDED, LANES), F32),
            pltpu.VMEM((PADDED, LANES), F32),
            pltpu.VMEM((GROUPS + 4, 2, LANES), F32),
            pltpu.VMEM((GROUPS + 4, 2, LANES), F32),
            pltpu.VMEM((4, LANES), F32),
            pltpu.VMEM((PADDED, LANES), F32),
            pltpu.VMEM((SERVERS, 4, LANES), BF16),
            pltpu.VMEM((SERVERS, 4, LANES), BF16),
            pltpu.VMEM((4, LANES), BF16),
            pltpu.VMEM((2, 4, 8, 8, 4, LANES), BF16),
            pltpu.VMEM((16, 32, LANES), F32),
            dma((10,)), dma((2,)), dma((4,)), dma((4,)), dma((3,)), dma((3,)),
            pltpu.SemaphoreType.REGULAR,
            dma, dma, dma, dma((8,)), dma, dma((3,)), dma, dma,
        ],
        compiler_params=pltpu.CompilerParams(
            collective_id=0, has_side_effects=True, vmem_limit_bytes=60 * 1024 * 1024
        ),
        cost_estimate=pl.CostEstimate(flops=2 * 128 * 16 * FF, bytes_accessed=5_000_000, transcendentals=2 * FF),
        name="compressed_step",
    )(
        hidden[0],
        cotangent[0].T,
        grouped(momentum),
        grouped(worker_error),
        server_error,
        grouped(master),
        grouped(second_moment),
    )

    moment, werr, serr, weights = pl.pallas_call(
        finish,
        out_shape=[jax.ShapeDtypeStruct(a.shape, a.dtype) for a in (moment, werr, serr, weights)],
        in_specs=[anywhere] * 4,
        out_specs=[anywhere] * 4,
        scratch_shapes=[dma((4,))],
        compiler_params=pltpu.CompilerParams(vmem_limit_bytes=1024 * 1024),
        name="finish",
    )(moment, werr, serr, weights)

    def rows_of(a):
        return a.transpose(1, 0, 2).reshape(1, 2, FF)

    return rows_of(moment), rows_of(werr), serr, weights


def solution(mesh):
    in_specs = (
        P("dp", "node", None),
        P("dp", "node", None),
        P("dp", "node", None),
        P("dp", "node", None),
        P("node", "dp"),
        P("node", None),
        P("node", None),
    )
    out_specs = (P("dp", "node", None), P("dp", "node", None), P("node", "dp"), P())
    return jax.shard_map(body, mesh=mesh, in_specs=in_specs, out_specs=out_specs, check_vma=False)
```

```python
import functools

import jax
import jax.numpy as jnp
from jax import lax
from jax.experimental import pallas as pl
from jax.experimental.pallas import tpu as pltpu
from jax.sharding import PartitionSpec as P

MESH = pl.DeviceIdType.MESH
F32 = jnp.float32
BF16 = jnp.bfloat16

FF = 13824
LANES = 128
GROUPS = FF // LANES
DENSE = 2 * GROUPS
PADDED = 224
SERVERS = 64
PIECE = FF // SERVERS
QUARTER = GROUPS // 4
BETA = 0.9
EPSILON = 1e-6
RATE = 0.5


def far_first(j, half):
    odd = lax.rem(j, 2)
    return half + (1 - odd) * (j // 2) - odd * ((j + 1) // 2)


def device(x, y, z, c):
    return ((y // 2) * 2 + c, z * 8 + lax.rem(y, 2) * 4 + x)


def kernel(
    hid, cot, mom, werr, serr, mast, second,
    moment_out, werr_out, serr_out, weights_out,
    cot_v, serr_raw, hid_v, part, core_out, core_in, y_out, y_in, mom_v, werr_v, mast_v, second_v, serr_v,
    sent_v, pieces, arrived, wpiece, gathered, wall, spread,
    load_sem, store_sem, core_send, core_recv, y_send, y_recv, ready,
    b_send, b_recv, c_send, c_recv, x_send, x_recv, s_send, s_recv,
):
    node = lax.axis_index("node")
    dp = lax.axis_index("dp")
    c = lax.rem(node, 2)
    yh = node // 2
    z = dp // 8
    yl = lax.rem(dp // 4, 2)
    x = lax.rem(dp, 4)
    y = yh * 2 + yl
    sibling = (node + 1 - 2 * c, dp)

    loads = [
        pltpu.make_async_copy(
            hid.at[:, pl.ds(j * QUARTER * LANES, QUARTER * LANES)],
            hid_v.at[:, pl.ds(j * QUARTER * LANES, QUARTER * LANES)],
            load_sem.at[j],
        )
        for j in range(4)
    ]
    states = [
        pltpu.make_async_copy(mom.reshape(DENSE, LANES), mom_v.at[pl.ds(0, DENSE)], load_sem.at[4]),
        pltpu.make_async_copy(werr.reshape(DENSE, LANES), werr_v.at[pl.ds(0, DENSE)], load_sem.at[5]),
        pltpu.make_async_copy(mast, mast_v.at[pl.ds(0, GROUPS)], load_sem.at[6]),
        pltpu.make_async_copy(second, second_v.at[pl.ds(0, GROUPS)], load_sem.at[7]),
        pltpu.make_async_copy(serr, serr_raw, load_sem.at[8]),
    ]
    barrier = pltpu.get_barrier_semaphore()

    def greet(who):
        pl.semaphore_signal(barrier, 1, device_id=who, device_id_type=MESH)

    for d in (4, 2, 6):
        greet(device(x, lax.rem(y + d, 8), z, c))
    greet(sibling)
    cot_load = pltpu.make_async_copy(cot, cot_v, load_sem.at[9])
    cot_load.start()
    for load in loads:
        load.start()
    for d in (4, 3, 5, 2, 6, 1, 7):
        greet(device(x, y, lax.rem(z + d, 8), c))
    for d in (3, 5, 1, 7):
        greet(device(x, lax.rem(y + d, 8), z, c))
    for d in (2, 1, 3):
        greet(device(lax.rem(x + d, 4), yh * 2 + 1 - yl, z, c))
        greet(device(lax.rem(x + d, 4), y, z, c))

    for state in states:
        state.start()

    tail = jnp.zeros((PADDED - DENSE, LANES), F32)
    for a in range(2):
        for b in range(4):
            part[a, b, pl.ds(DENSE, PADDED - DENSE), :] = tail
    mom_v[pl.ds(DENSE, PADDED - DENSE), :] = tail
    werr_v[pl.ds(DENSE, PADDED - DENSE), :] = tail
    mast_v[pl.ds(GROUPS, 4)] = jnp.zeros((4, 2, LANES), F32)
    second_v[pl.ds(GROUPS, 4)] = jnp.zeros((4, 2, LANES), F32)
    serr_v[...] = jnp.zeros((4, LANES), F32)

    cot_load.wait()
    cot_value = cot_v[...]
    for j in range(4):
        loads[j].wait()
        sums = jnp.dot(
            cot_value,
            hid_v[:, pl.ds(j * QUARTER * LANES, QUARTER * LANES)],
            preferred_element_type=F32,
        )
        for g in range(QUARTER):
            row = 2 * (j * QUARTER + g)
            for n in range(8):
                part[n % 2, n // 2, pl.ds(row, 2), :] = sums[
                    2 * n : 2 * n + 2, g * LANES : (g + 1) * LANES
                ]

    for d in range(4):
        core_out[d] = part[1 - c, lax.rem(yh + d, 4)].astype(BF16)
    pl.semaphore_wait(barrier, 21)

    def to_core(d):
        return pltpu.make_async_remote_copy(
            core_out.at[d], core_in.at[d], core_send.at[d], core_recv.at[d],
            device_id=sibling, device_id_type=MESH,
        )

    def to_node(d):
        return pltpu.make_async_remote_copy(
            y_out.at[d - 1], y_in.at[d - 1], y_send.at[d - 1], y_recv.at[d - 1],
            device_id=(lax.rem(yh + d, 4) * 2 + c, dp), device_id_type=MESH,
        )

    for d in (2, 1, 3, 0):
        to_core(d).start()

    for d in (2, 1, 3):
        to_core(d).wait_recv()
        y_out[d - 1] = (part[c, lax.rem(yh + d, 4)] + core_in[d].astype(F32)).astype(BF16)
        to_node(d).start()
    for d in (4, 3, 5, 2, 6, 1, 7):
        pl.semaphore_signal(
            ready, 1, device_id=device(x, y, lax.rem(z + d, 8), c), device_id_type=MESH
        )
    to_core(0).wait_recv()
    gradient = part[c, yh] + core_in[0].astype(F32)
    states[0].wait()
    states[1].wait()
    for d in (1, 3, 2):
        to_node(d).wait_recv()
        gradient = gradient + y_in[d - 1].astype(F32)

    moment = BETA * mom_v[...] + (1.0 - BETA) * gradient
    carried = moment + werr_v[...]
    mom_v[...] = moment
    square = jnp.sum(carried * carried, axis=(0, 1), keepdims=True)
    scale = jnp.sqrt(square / (2 * FF) + EPSILON)
    sent = (scale * jnp.tanh(carried * (1.0 / scale))).astype(BF16).astype(F32)
    sent_v[...] = sent
    werr_v[...] = carried - sent

    lane = lax.broadcasted_iota(jnp.int32, (8, LANES), 1)
    for p in range(SERVERS):
        group, shift = divmod(PIECE * p, LANES)
        rows = sent_v[pl.ds(2 * group, 8), :]
        if shift:
            first = pltpu.roll(rows, LANES - shift, 1)
            rows = jnp.where(lane < LANES - shift, first, pltpu.roll(first, 6, 0))
        pieces[p] = rows[0:4]

    pl.semaphore_wait(ready, 7)

    def to_server(k):
        jz, jx, jy = k // 8, lax.rem(k, 8) // 2, lax.rem(k, 2)
        tz = lax.rem(z + far_first(jz, 4), 8)
        tx = lax.rem(x + far_first(jx, 2), 4)
        ty = lax.rem(yl + 1 - jy, 2)
        target = tz * 8 + ty * 4 + tx
        return pltpu.make_async_remote_copy(
            pieces.at[target], arrived.at[dp], b_send, b_recv, device_id=(node, target), device_id_type=MESH
        )

    @pl.loop(0, SERVERS - 1, unroll=21)
    def _(k):
        to_server(k).start()

    arrived[dp] = pieces[dp]
    moment_store = pltpu.make_async_copy(mom_v.at[pl.ds(0, DENSE)], moment_out.reshape(DENSE, LANES), store_sem.at[0])
    werr_store = pltpu.make_async_copy(werr_v.at[pl.ds(0, DENSE)], werr_out.reshape(DENSE, LANES), store_sem.at[1])
    moment_store.start()
    werr_store.start()

    states[2].wait()
    states[3].wait()
    states[4].wait()
    serr_v[pl.ds(0, 2), :] = serr_raw[:, pl.ds(0, LANES)]
    serr_v[pl.ds(2, 2), pl.ds(0, PIECE - LANES)] = serr_raw[:, pl.ds(LANES, PIECE - LANES)]
    column = dp * PIECE
    group, shift = column // LANES, lax.rem(column, LANES)

    def own_piece(ref):
        rows = jnp.concatenate([ref[group + j] for j in range(4)], axis=0)
        first = pltpu.roll(rows, lax.rem(LANES - shift, LANES), 1)
        return jnp.where(lane < LANES - shift, first, pltpu.roll(first, 6, 0))[0:4]

    row4 = lax.broadcasted_iota(jnp.int32, (4, LANES), 0)
    lane4 = lax.broadcasted_iota(jnp.int32, (4, LANES), 1)
    valid = (row4 < 2) | (lane4 < PIECE - LANES)
    own_master = own_piece(mast_v)
    step = RATE / (jnp.sqrt(jnp.where(valid, own_piece(second_v), 1.0)) + 1e-8)

    others = pl.ds(0, SERVERS - 1)
    pltpu.make_async_copy(arrived.at[others], arrived.at[others], b_recv).wait()
    served = jnp.sum(arrived[...], axis=0) / SERVERS + serr_v[...]
    served = jnp.where(valid, served, 0.0)
    square = jnp.sum(served * served, axis=(0, 1), keepdims=True)
    scale = jnp.sqrt(square / (2 * PIECE) + EPSILON)
    returned = (scale * jnp.tanh(served / scale)).astype(BF16).astype(F32)
    updated = own_master - step * returned
    updated = jnp.concatenate([updated[0:1], updated[2:3], updated[1:2], updated[3:4]], axis=0)
    wpiece[...] = updated.astype(BF16).astype(F32)

    slot = yl * 4 + yh

    def to_plane(k):
        dz = far_first(k // 8, 4)
        ty = lax.rem(y + far_first(lax.rem(k, 8), 4), 8)
        return pltpu.make_async_remote_copy(
            wpiece, gathered.at[z, slot], c_send, c_recv.at[dz],
            device_id=device(x, ty, lax.rem(z + dz, 8), c), device_id_type=MESH,
        )

    @pl.loop(0, SERVERS - 1, unroll=21)
    def _(k):
        to_plane(k).start()

    gathered[z, slot] = wpiece[...]
    residual = served - returned
    serr_out[:, pl.ds(0, LANES)] = residual[0:2]
    serr_out[:, pl.ds(LANES, PIECE - LANES)] = residual[2:4, 0 : PIECE - LANES]

    def to_x(d, source):
        block = wall.at[c, x, source]
        return pltpu.make_async_remote_copy(
            block, block, x_send, x_recv.at[d - 1],
            device_id=(node, dp - x + lax.rem(x + d, 4)), device_id_type=MESH,
        )

    def to_sibling(block):
        return pltpu.make_async_remote_copy(
            block, block, s_send, s_recv, device_id=sibling, device_id_type=MESH
        )

    for dz in (0, 1, 7, 2, 6, 3, 5, 4):
        source = lax.rem(z + 8 - dz, 8)
        landed = gathered.at[source, pl.ds(0, 8 if dz else 7)]
        pltpu.make_async_copy(landed, landed, c_recv.at[dz]).wait()
        wall[c, x, source] = gathered[source].reshape(32, LANES).astype(BF16)
        for d in (2, 1, 3):
            to_x(d, source).start()
        to_sibling(wall.at[c, x, source]).start()
    for d in (1, 3, 2):
        block = wall.at[c, lax.rem(x + 4 - d, 4)]
        pltpu.make_async_copy(block, block, x_recv.at[d - 1]).wait()
        to_sibling(block).start()
    pltpu.make_async_copy(wall.at[1 - c], wall.at[1 - c], s_recv).wait()

    @pl.loop(0, 4)
    def _(q):
        parts = [[] for _ in range(QUARTER)]
        for pp in range(16):
            for core in range(2):
                block = wall[core, pp % 4, 2 * q + pp // 8, pl.ds(16 * (pp // 4 % 2), 16), :].astype(F32)
                for h in range(4):
                    spread[pp, pl.ds(8 * h + 4 * core, 4), :] = block[4 * h : 4 * h + 4]
            for half in range(2):
                rows = [spread[pp, pl.ds(16 * h + half, 8, stride=2), :] for h in range(2)]
                begin = PIECE * pp + LANES * half
                end = min(begin + LANES, PIECE * (pp + 1))
                group, shift = divmod(begin, LANES)
                if shift:
                    rows = [pltpu.roll(r, shift, 1) for r in rows]
                for g in (group, group + 1):
                    if max(begin, g * LANES) < min(end, (g + 1) * LANES):
                        parts[g].append((max(begin, g * LANES) - g * LANES, rows))
        for g in range(QUARTER):
            total = parts[g][0][1]
            for low, rows in parts[g][1:]:
                total = [jnp.where(lane < low, t, r) for t, r in zip(total, rows)]
            weights_out[:, pl.ds(pl.multiple_of(q * QUARTER * LANES + g * LANES, LANES), LANES)] = (
                jnp.concatenate(total, axis=0).astype(BF16)
            )

    moment_store.wait()
    werr_store.wait()
    for d in range(4):
        to_core(d).wait_send()
    for d in range(1, 4):
        to_node(d).wait_send()
    pltpu.make_async_copy(arrived.at[others], arrived.at[others], b_send).wait()
    pltpu.make_async_copy(arrived.at[others], arrived.at[others], c_send).wait()
    pltpu.make_async_copy(wall.at[c, pl.ds(0, 3)], wall.at[c, pl.ds(0, 3)], x_send).wait()
    pltpu.make_async_copy(wall.at[c], wall.at[c], s_send).wait()


def finish(*refs):
    sems = refs[8]
    copies = [pltpu.make_async_copy(refs[i], refs[4 + i], sems.at[i]) for i in (3, 0, 1, 2)]
    for copy in copies:
        copy.start()
    for copy in copies:
        copy.wait()


def grouped(a):
    return a.reshape(2, GROUPS, LANES).transpose(1, 0, 2)


def body(hidden, cotangent, momentum, worker_error, server_error, master, second_moment):
    anywhere = pl.BlockSpec(memory_space=pl.ANY)
    vmem = pl.BlockSpec(memory_space=pltpu.VMEM)
    dma = pltpu.SemaphoreType.DMA
    moment, werr, serr, weights = pl.pallas_call(
        kernel,
        out_shape=[
            pltpu.VMEM((GROUPS, 2, LANES), F32),
            pltpu.VMEM((GROUPS, 2, LANES), F32),
            pltpu.VMEM((2, PIECE), F32),
            pltpu.VMEM((16, FF), BF16),
        ],
        in_specs=[anywhere] * 7,
        out_specs=[anywhere, anywhere, vmem, vmem],
        scratch_shapes=[
            pltpu.VMEM((16, 128), BF16),
            pltpu.VMEM((2, PIECE), F32),
            pltpu.VMEM((128, FF), BF16),
            pltpu.VMEM((2, 4, PADDED, LANES), F32),
            pltpu.VMEM((4, PADDED, LANES), BF16),
            pltpu.VMEM((4, PADDED, LANES), BF16),
            pltpu.VMEM((3, PADDED, LANES), BF16),
            pltpu.VMEM((3, PADDED, LANES), BF16),
            pltpu.VMEM((PADDED, LANES), F32),
            pltpu.VMEM((PADDED, LANES), F32),
            pltpu.VMEM((GROUPS + 4, 2, LANES), F32),
            pltpu.VMEM((GROUPS + 4, 2, LANES), F32),
            pltpu.VMEM((4, LANES), F32),
            pltpu.VMEM((PADDED, LANES), F32),
            pltpu.VMEM((SERVERS, 4, LANES), F32),
            pltpu.VMEM((SERVERS, 4, LANES), F32),
            pltpu.VMEM((4, LANES), F32),
            pltpu.VMEM((8, 8, 4, LANES), F32),
            pltpu.VMEM((2, 4, 8, 32, LANES), BF16),
            pltpu.VMEM((16, 32, LANES), F32),
            dma((10,)), dma((2,)), dma((4,)), dma((4,)), dma((3,)), dma((3,)),
            pltpu.SemaphoreType.REGULAR,
            dma, dma, dma, dma((8,)), dma, dma((3,)), dma, dma,
        ],
        compiler_params=pltpu.CompilerParams(
            collective_id=0, has_side_effects=True, vmem_limit_bytes=60 * 1024 * 1024
        ),
        cost_estimate=pl.CostEstimate(flops=2 * 128 * 16 * FF, bytes_accessed=5_000_000, transcendentals=2 * FF),
        name="compressed_step",
    )(
        hidden[0],
        cotangent[0].T,
        grouped(momentum),
        grouped(worker_error),
        server_error,
        grouped(master),
        grouped(second_moment),
    )

    moment, werr, serr, weights = pl.pallas_call(
        finish,
        out_shape=[jax.ShapeDtypeStruct(a.shape, a.dtype) for a in (moment, werr, serr, weights)],
        in_specs=[anywhere] * 4,
        out_specs=[anywhere] * 4,
        scratch_shapes=[dma((4,))],
        compiler_params=pltpu.CompilerParams(vmem_limit_bytes=1024 * 1024),
        name="finish",
    )(moment, werr, serr, weights)

    def rows_of(a):
        return a.transpose(1, 0, 2).reshape(1, 2, FF)

    return rows_of(moment), rows_of(werr), serr, weights


def solution(mesh):
    in_specs = (
        P("dp", "node", None),
        P("dp", "node", None),
        P("dp", "node", None),
        P("dp", "node", None),
        P("node", "dp"),
        P("node", None),
        P("node", None),
    )
    out_specs = (P("dp", "node", None), P("dp", "node", None), P("node", "dp"), P())
    return jax.shard_map(body, mesh=mesh, in_specs=in_specs, out_specs=out_specs, check_vma=False)
```
